32 devices in a mesh: prog: 32 (over z, y, x, core), clus: 1.
Axes of the slice: x: 2, y: 2, z: 4, core: 2. Of those that a mesh axis runs over, the one named last changes fastest.
Arguments:
- embeddings: bfloat16 [32768, 2048], P('prog', 'clus'), may hold values from -64 to 64, as said below
- centroids: bfloat16 [4096, 2048], P('clus'), may hold values from -6 to 6, as said below
- plan_grad: bfloat16 [32768, 4096], P('prog', 'clus'), may hold values from -24 to 24
Outputs:
- embed_grad: bfloat16 [32768, 2048], P('prog', 'clus')
- centroid_grad: bfloat16 [4096, 2048], P(('clus', 'prog'))
The draws below stay inside these ranges and needn't reach their ends.
Inputs may be any that keep to these rules, and one draw needn't show every extreme that they name: embeddings are real-valued with full-rank spread. centroids are real-valued with full-rank spread.
All inputs are finite; a program needn't handle non-finite values.
Results may differ from the reference program's by a relative error of at most 0.006.
Values may be sent and summed in bfloat16 or wider, within the bound.
A program may use at most 128 MiB of HBM per device.

```python
import jax
import jax.numpy as jnp
from jax import lax

D = 2048
CENTROIDS = 4096
ITERS = 4
TOTAL = 32768


def draw_common(key):
    cent = jnp.clip(jax.random.normal(jax.random.fold_in(key, 7), (CENTROIDS, D), jnp.float32), -6.0, 6.0)
    embed = 2.0 * jnp.clip(jax.random.normal(jax.random.fold_in(key, 11), (TOTAL, D), jnp.float32), -6.0, 6.0)
    dead = jax.random.randint(jax.random.fold_in(key, 29), (), 0, CENTROIDS)
    cent = cent.at[dead].set(-6.0)
    aligned = min(64, TOTAL // 2)
    pick_one = jax.random.randint(jax.random.fold_in(key, 19), (aligned,), 1, CENTROIDS)
    offset = jax.random.randint(jax.random.fold_in(key, 23), (aligned,), 1, CENTROIDS - 1)
    pick_two = 1 + (pick_one - 1 + offset) % (CENTROIDS - 1)
    first = (dead + pick_one) % CENTROIDS
    second = (dead + pick_two) % CENTROIDS
    strength = jnp.array([0.6, 0.9, 1.2], jnp.float32)[jnp.arange(aligned) % 3][:, None]
    lift = 50.0 / jnp.sqrt(jnp.float32(D))
    mixed = strength * (cent[first] + 0.99 * cent[second]) * lift
    embed = embed.at[:aligned].set(mixed)
    embed = jnp.clip(embed + 2.0, -64.0, 64.0)
    return (embed, cent)


def draw_embeddings(key, part):
    return draw_common(key)[0].astype(jnp.bfloat16)


def draw_centroids(key, part):
    return draw_common(key)[1].astype(jnp.bfloat16)


def strengthened(result, stream_key, source, target, parts, factor):
    def block_of(position):
        return (jnp.arange(result.shape[position]) // (result.shape[position] // parts)).reshape((-1,) + (1,) * (result.ndim - 1 - position))

    one_side = jax.random.permutation(stream_key, parts)[block_of(target)]
    far = (block_of(target) + parts // 2) % parts
    return jnp.where((block_of(source) == one_side) | (block_of(source) == far), factor * result, result)


def block_levels(stream_key, extent, split, low, top_value):
    def one(dim, blocks):
        steps = jax.random.uniform(jax.random.fold_in(jax.random.fold_in(stream_key, 6), dim), (blocks,), jnp.float32, low / len(split), top_value / len(split))
        return jnp.repeat(jnp.exp(steps), extent[dim] // blocks).reshape((-1,) + (1,) * (len(extent) - dim - 1))

    factor_of = one(*split[0])
    for cut in split[1:]:
        factor_of = factor_of * one(*cut)
    return factor_of


def noise_with(rng, dims, width, most, cuts, heavy, kind=jnp.bfloat16):
    entries = width * jax.random.normal(rng, dims, jnp.float32)
    if cuts:
        entries = entries * block_levels(rng, dims, cuts, -0.22, 0.18)
    return jnp.clip(strengthened(entries, jax.random.fold_in(rng, 3), *heavy), -most, most).astype(kind)


def setup_inputs(seed: int = 0) -> dict:
    splits = jax.random.split(jax.random.key(seed), 4)
    return {
        "embeddings": draw_embeddings(jax.random.fold_in(splits[3], 71), 0),
        "centroids": draw_centroids(jax.random.fold_in(splits[3], 71), 0),
        "plan_grad": noise_with(splits[2], (TOTAL, CENTROIDS), 4.0, 24.0, ((0, 32),), (0, 1, 32, 2.75)),
    }


def lse_along(values, axis):
    top = lax.optimization_barrier(jnp.max(values, axis=axis, keepdims=True))
    total = lax.optimization_barrier(jnp.sum(jnp.exp(values - top), axis=axis, keepdims=True))
    return jnp.squeeze(top + jnp.log(total), axis)

def reference(embeddings, centroids, plan_grad):
    scale = 1.0 / (0.25 * jnp.sqrt(jnp.float32(D)))
    logits = scale * lax.dot_general(embeddings, centroids, (((1,), (1,)), ((), ())), preferred_element_type=jnp.float32)
    log_b = jnp.log(jnp.float32(TOTAL) / jnp.float32(CENTROIDS))
    col_pot = jnp.zeros((CENTROIDS,), jnp.float32)
    row_list = []
    col_list = []
    for step in range(ITERS):
        row_pot = -lse_along(logits + col_pot[None, :], 1)
        col_pot = log_b - lse_along(logits + row_pot[:, None], 0)
        row_list.append(row_pot)
        col_list.append(col_pot)
    plan = jnp.exp(logits + row_list[-1][:, None] + col_list[-1][None, :])
    pbar = plan_grad.astype(jnp.float32) * plan
    adjoint = pbar
    col_adj = lax.optimization_barrier(jnp.sum(pbar, axis=0))
    direct = lax.optimization_barrier(jnp.sum(pbar, axis=1))
    for step in range(ITERS - 1, -1, -1):
        weights_a = jnp.exp(logits + row_list[step][:, None] + col_list[step][None, :] - log_b)
        term_a = weights_a * col_adj[None, :]
        adjoint = adjoint - term_a
        row_adj = direct - lax.optimization_barrier(jnp.sum(term_a, axis=1))
        direct = jnp.zeros_like(direct)
        if step > 0:
            prev_col = col_list[step - 1]
        else:
            prev_col = jnp.zeros((CENTROIDS,), jnp.float32)
        term_b = jnp.exp(logits + prev_col[None, :] + row_list[step][:, None]) * row_adj[:, None]
        adjoint = adjoint - term_b
        if step > 0:
            col_adj = -lax.optimization_barrier(jnp.sum(term_b, axis=0))
    adjoint_b = adjoint.astype(jnp.bfloat16)
    embed_grad = (scale * jnp.dot(adjoint_b, centroids, preferred_element_type=jnp.float32)).astype(jnp.bfloat16)
    centroid_grad = (scale * lax.dot_general(adjoint_b, embeddings, (((0,), (0,)), ((), ())), preferred_element_type=jnp.float32)).astype(jnp.bfloat16)
    return (embed_grad, centroid_grad)
```

```python
import functools

import jax
import jax.numpy as jnp
from jax import lax
from jax.experimental import pallas as pl
from jax.experimental.pallas import tpu as pltpu
from jax.sharding import PartitionSpec as P

ITERS = 4


def merged(part, axis, combine):
    gathered = jax.tree.map(lambda a: lax.all_gather(a, axis), part)

    def take(source):
        return jax.tree.map(lambda a: lax.dynamic_index_in_dim(a, source, 0, False), gathered)

    return lax.fori_loop(
        1, lax.axis_size(axis), lambda source, state: combine(state, take(source)), take(0)
    )


def lse_combine(first, second):
    top = jnp.maximum(first[0], second[0])
    total = first[1] * jnp.exp(first[0] - top) + second[1] * jnp.exp(second[0] - top)
    return (top, total)


def row_lse(values):
    local_top = jnp.max(values, axis=1)
    local_total = jnp.sum(jnp.exp(values - local_top[:, None]), axis=1)
    top, total = merged((local_top, local_total), "clus", lse_combine)
    return top + jnp.log(total)


def col_lse(values):
    local_top = jnp.max(values, axis=0)
    local_total = jnp.sum(jnp.exp(values - local_top[None, :]), axis=0)
    top, total = merged((local_top, local_total), "prog", lse_combine)
    return top + jnp.log(total)


def general_shards(embeddings, centroids, plan_grad):
    scale = 1.0 / (0.25 * jnp.sqrt(jnp.float32(embeddings.shape[1] * lax.axis_size("clus"))))
    whole_rows = lax.all_gather(embeddings, "clus", axis=1, tiled=True)
    logits = scale * lax.dot_general(
        whole_rows, centroids, (((1,), (1,)), ((), ())), preferred_element_type=jnp.float32
    )
    total_rows = embeddings.shape[0] * lax.axis_size("prog")
    log_b = jnp.log(jnp.float32(total_rows) / jnp.float32(centroids.shape[0] * lax.axis_size("clus")))
    col_pot = jnp.zeros((centroids.shape[0],), jnp.float32)
    row_list = []
    col_list = []
    for step in range(ITERS):
        row_pot = -row_lse(logits + col_pot[None, :])
        col_pot = log_b - col_lse(logits + row_pot[:, None])
        row_list.append(row_pot)
        col_list.append(col_pot)
    plan = jnp.exp(logits + row_list[-1][:, None] + col_list[-1][None, :])
    pbar = plan_grad.astype(jnp.float32) * plan
    adjoint = pbar
    col_adj = lax.psum(jnp.sum(pbar, axis=0), "prog")
    direct = jnp.sum(pbar, axis=1)
    for step in range(ITERS - 1, -1, -1):
        weights_a = jnp.exp(logits + row_list[step][:, None] + col_list[step][None, :] - log_b)
        term_a = weights_a * col_adj[None, :]
        adjoint = adjoint - term_a
        row_adj = lax.psum(direct - jnp.sum(term_a, axis=1), "clus")
        direct = jnp.zeros_like(direct)
        if step > 0:
            prev_col = col_list[step - 1]
        else:
            prev_col = jnp.zeros_like(col_pot)
        term_b = jnp.exp(logits + prev_col[None, :] + row_list[step][:, None]) * row_adj[:, None]
        adjoint = adjoint - term_b
        if step > 0:
            col_adj = -lax.psum(jnp.sum(term_b, axis=0), "prog")
    adjoint_b = adjoint.astype(jnp.bfloat16)
    partial_rows = scale * jnp.dot(adjoint_b, centroids, preferred_element_type=jnp.float32)
    embed_grad = lax.psum_scatter(partial_rows, "clus", scatter_dimension=1, tiled=True).astype(
        jnp.bfloat16
    )
    centroid_grad = lax.psum_scatter(
        scale
        * lax.dot_general(
            adjoint_b, whole_rows, (((0,), (0,)), ((), ())), preferred_element_type=jnp.float32
        ),
        "prog",
        scatter_dimension=0,
        tiled=True,
    ).astype(jnp.bfloat16)
    return (embed_grad, centroid_grad)


LANES = 128
MESH_AXIS = "prog"


def sinkhorn_kernel(
    n, scale, ratio, emb, cent, grad, out,
    E, G, tiles, A, X, R, U, sub, cols, RW, RH, LH,
    send1, got1, reply1, back1, send2, got2, reply2, back2,
    tile_sem, grad_sem, out_sem, ss1, rs1, ss2, rs2,
):
    rows, C = E.shape
    W = C // n
    K = C // LANES
    me = lax.axis_index(MESH_AXIS)
    f32 = jnp.float32

    def other(k):
        return lax.rem(me + k, n)

    barrier = pltpu.get_barrier_semaphore()

    @pl.loop(1, n)
    def _(k):
        pl.semaphore_signal(barrier, inc=1, device_id={MESH_AXIS: other(k)},
                            device_id_type=pl.DeviceIdType.MESH)

    grad_copy = pltpu.make_async_copy(grad, G, grad_sem)
    width = tiles.shape[1]
    count = C // width

    def fetch(j):
        return pltpu.make_async_copy(
            cent.at[pl.ds(j * width, width), :], tiles.at[j % 2], tile_sem.at[j % 2])

    fetch(0).start()
    for j in range(count):
        if j + 1 < count:
            fetch(j + 1).start()
        if j == 0:
            grad_copy.start()
        fetch(j).wait()

        half = rows // 4

        @pl.loop(0, 4)
        def _(q, j=j):
            r0 = pl.multiple_of(q * half, half)
            E[pl.ds(r0, half), j * width:(j + 1) * width] = scale * lax.dot_general(
                emb[pl.ds(r0, half), :], tiles[j % 2], (((1,), (1,)), ((), ())),
                preferred_element_type=f32)

    pl.semaphore_wait(barrier, n - 1)

    BR = 64
    BC = 16
    CH = 8

    def rows_loop(body):
        @pl.loop(0, rows // BR)
        def _(i):
            body(pl.ds(pl.multiple_of(i * BR, BR), BR))

    def lane(k):
        return slice(k * LANES, (k + 1) * LANES)

    def cols_loop(body, init, outs, combine):
        for c in range(K // CH):
            def step(i, accs, c=c):
                r = pl.ds(pl.multiple_of(i * BC, BC), BC)
                new = []
                for q in range(CH):
                    terms = body(r, c * CH + q)
                    new.append(tuple(combine(a, t) for a, t in zip(accs[q], terms)))
                return tuple(new)

            start = tuple(
                tuple(jnp.full((BC, LANES), init, f32) for _ in outs) for _ in range(CH))
            accs = lax.fori_loop(0, rows // BC, step, start, unroll=2)
            for q in range(CH):
                for o, a in zip(outs, accs[q]):
                    if combine is jnp.maximum:
                        red = jnp.max(a, axis=0, keepdims=True)
                    else:
                        red = jnp.sum(a, axis=0, keepdims=True)
                    o[:, lane(c * CH + q)] = red

    def total(part):
        return jnp.broadcast_to(jnp.sum(part, axis=1, keepdims=True), part.shape)

    def row_pass(y):
        def body(r):
            acc = E[r, lane(0)] * y[:, lane(0)]
            for k in range(1, K):
                acc = acc + E[r, lane(k)] * y[:, lane(k)]
            R[r, :] = acc
        rows_loop(body)

    def exchange(vectors, combine, results, send, got, reply, back):
        for k in range(n):
            for q, v in enumerate(vectors):
                send[k, :, q * W:(q + 1) * W] = v[:, k * W:(k + 1) * W]

        def first(k):
            t = other(k)
            return pltpu.make_async_remote_copy(
                src_ref=send.at[t], dst_ref=got.at[me], send_sem=ss1.at[t],
                recv_sem=rs1.at[me], device_id={MESH_AXIS: t},
                device_id_type=pl.DeviceIdType.MESH)

        def first_in(k):
            t = other(k)
            return pltpu.make_async_remote_copy(
                src_ref=send.at[t], dst_ref=got.at[t], send_sem=ss1.at[t],
                recv_sem=rs1.at[t], device_id={MESH_AXIS: t},
                device_id_type=pl.DeviceIdType.MESH)

        def second(k):
            t = other(k)
            return pltpu.make_async_remote_copy(
                src_ref=reply, dst_ref=back.at[me], send_sem=ss2.at[t],
                recv_sem=rs2.at[me], device_id={MESH_AXIS: t},
                device_id_type=pl.DeviceIdType.MESH)

        def second_in(k):
            t = other(k)
            return pltpu.make_async_remote_copy(
                src_ref=reply, dst_ref=back.at[t], send_sem=ss2.at[t],
                recv_sem=rs2.at[t], device_id={MESH_AXIS: t},
                device_id_type=pl.DeviceIdType.MESH)

        @pl.loop(1, n)
        def _(k):
            first(k).start()

        got[me] = send[me]

        @pl.loop(1, n)
        def _(k):
            first_in(k).wait_recv()

        arrived = got[...]
        answers = combine([arrived[:, :, q * W:(q + 1) * W] for q in range(len(vectors))])
        for q, a in enumerate(answers):
            reply[:, q * W:(q + 1) * W] = a

        @pl.loop(1, n)
        def _(k):
            second(k).start()

        back[me] = reply[...]

        @pl.loop(1, n)
        def _(k):
            first(k).wait_send()
            second_in(k).wait_recv()

        for k in range(n):
            for q, v in enumerate(results):
                v[:, k * W:(k + 1) * W] = back[k, :, q * W:(q + 1) * W]

        @pl.loop(1, n)
        def _(k):
            second(k).wait_send()

    M, F = cols.at[pl.ds(0, 1)], cols.at[pl.ds(1, 1)]
    B = {t: cols.at[pl.ds(t, 1)] for t in (2, 3, 4)}
    DV = cols.at[pl.ds(5, 1)]
    Y, Y2, S, S2, EM = (cols.at[pl.ds(q, 1)] for q in (8, 9, 10, 11, 12))

    def top_body(r):
        acc = E[r, lane(0)]
        for k in range(1, K):
            acc = jnp.maximum(acc, E[r, lane(k)])
        R[r, :] = jnp.broadcast_to(jnp.max(acc, axis=1, keepdims=True), acc.shape)

    rows_loop(top_body)

    def exp_body(r):
        top = R[r, :]
        acc = jnp.exp(E[r, lane(0)] - top)
        for k in range(1, K):
            acc = acc + jnp.exp(E[r, lane(k)] - top)
        U[r, :] = -(top + jnp.log(total(acc)))

    rows_loop(exp_body)
    cols_loop(lambda r, k: [E[r, lane(k)] + U[r, :]], -jnp.inf, [M], jnp.maximum)

    def shift(r, k):
        e = jnp.exp(E[r, lane(k)] + U[r, :] - M[:, lane(k)])
        E[r, lane(k)] = e
        return [e]

    add = lambda a, b: a + b
    cols_loop(shift, 0.0, [S], add)

    def lse(parts):
        m, s = parts
        top = jnp.max(m, axis=0)
        whole = jnp.sum(s * jnp.exp(m - top[None]), axis=0)
        v = jnp.log(f32(ratio)) - (top + jnp.log(whole))
        return [v, v]

    exchange([M, S], lse, [Y], send2, got2, reply2, back2)
    F[...] = jnp.exp(M[...] + Y[...])
    EM[...] = jnp.exp(M[...])

    def plain(parts):
        return [jnp.sum(p, axis=0) for p in parts]

    def fb(t):
        if t == 0:
            return EM[...]
        return F[...] if t == 1 else F[...] * B[t][...]

    A[0] = jnp.ones((rows, LANES), f32)
    for t in (2, 3, 4):
        Y[...] = fb(t - 1)
        row_pass(Y)
        A[t - 1] = 1.0 / total(R[...])
        if t < 4:
            cols_loop(lambda r, k, t=t: [E[r, lane(k)] * A[t - 1, r, :]], 0.0, [S], add)
            S[...] = S[...] * F[...]
            exchange([S], plain, [Y], send1, got1, reply1, back1)
            B[t][...] = ratio / Y[...]
        else:
            grad_copy.wait()

            def both(r, k):
                w = E[r, lane(k)] * A[3, r, :]
                return [w, w * G[r, lane(k)].astype(f32)]

            cols_loop(both, 0.0, [S, S2], add)
            S[...] = S[...] * F[...]
            S2[...] = S2[...] * F[...]
            exchange([S, S2], plain, [Y, Y2], send2, got2, reply2, back2)
            B[t][...] = ratio / Y[...]
            DV[...] = B[t][...] * Y2[...]

    for t in (4, 3, 2, 1):
        Y[...] = fb(t) * DV[...] * (1.0 / ratio)
        RW[t - 1:t, :] = Y[...]
        RW[3 + t:4 + t, :] = fb(t - 1)
        if t == 4:
            Y2[...] = fb(4)

            def grad_body(r):
                acc = jnp.zeros((BR, LANES), f32)
                for k in range(K):
                    acc = acc + E[r, lane(k)] * (
                        G[r, lane(k)].astype(f32) * Y2[:, lane(k)] - Y[:, lane(k)])
                R[r, :] = acc

            rows_loop(grad_body)
            X[t - 1] = A[t - 1] * A[t - 1] * total(R[...])
        else:
            row_pass(Y)
            X[t - 1] = -(A[t - 1] * A[t - 1]) * total(R[...])
        if t > 1:
            cols_loop(lambda r, k, t=t: [E[r, lane(k)] * X[t - 1, r, :]], 0.0, [S], add)
            S[...] = S[...] * F[...]
            exchange([S], plain, [Y], send1, got1, reply1, back1)
            if t == 2:
                DV[...] = -Y[...]
            else:
                DV[...] = -Y[...] * B[t - 1][...]

    high = RW[...].astype(jnp.bfloat16).astype(f32)
    low = RW[...] - high
    RH[...] = jnp.concatenate(
        [high, low, high, jnp.zeros_like(high)], axis=0).astype(jnp.bfloat16)
    spot = lax.broadcasted_iota(jnp.int32, (BR, LANES), 1)

    def left(r):
        acc = jnp.zeros((BR, LANES), f32)
        for q in range(8):
            v = A[q, r, :] if q < 4 else X[q - 4, r, :]
            hi = v.astype(jnp.bfloat16).astype(f32)
            acc = jnp.where((spot == q) | (spot == q + 8), hi, acc)
            acc = jnp.where(spot == q + 16, v - hi, acc)
        LH[r, :] = acc.astype(jnp.bfloat16)

    rows_loop(left)
    Y2[...] = fb(4)

    def finish(r):
        lhs = LH[r, :][:, 0:32]
        a4 = A[3, r, :]
        for k in range(0, K, 2):
            wide = slice(k * LANES, (k + 2) * LANES)
            coef = jnp.dot(lhs, RH[:, wide], preferred_element_type=f32)
            a = jnp.concatenate([a4, a4], axis=1)
            val = E[r, wide] * (G[r, wide].astype(f32) * a * Y2[:, wide] - coef)
            G[r, wide] = val.astype(jnp.bfloat16)

    rows_loop(finish)
    done = pltpu.make_async_copy(G, out, out_sem)
    done.start()
    done.wait()


def adjoint_of(n, scale, ratio, embeddings, centroids, plan_grad):
    rows, depth = embeddings.shape
    C = centroids.shape[0]
    W = C // n
    f32 = jnp.float32
    width = 512
    vm = pltpu.VMEM
    scratch = [
        vm((rows, C), f32), vm((rows, C), jnp.bfloat16), vm((2, width, depth), jnp.bfloat16),
        vm((4, rows, LANES), f32), vm((4, rows, LANES), f32), vm((rows, LANES), f32),
        vm((rows, LANES), f32), vm((8, LANES), f32), vm((16, C), f32),
        vm((8, C), f32), vm((32, C), jnp.bfloat16), vm((rows, LANES), jnp.bfloat16),
        vm((n, 1, W), f32), vm((n, 1, W), f32), vm((1, W), f32), vm((n, 1, W), f32),
        vm((n, 1, 2 * W), f32), vm((n, 1, 2 * W), f32), vm((1, 2 * W), f32),
        vm((n, 1, 2 * W), f32),
        pltpu.SemaphoreType.DMA((2,)), pltpu.SemaphoreType.DMA, pltpu.SemaphoreType.DMA,
        pltpu.SemaphoreType.DMA((n,)), pltpu.SemaphoreType.DMA((n,)),
        pltpu.SemaphoreType.DMA((n,)), pltpu.SemaphoreType.DMA((n,)),
    ]
    return pl.pallas_call(
        functools.partial(sinkhorn_kernel, n, scale, ratio),
        out_shape=jax.ShapeDtypeStruct((rows, C), jnp.bfloat16),
        in_specs=[pl.BlockSpec(memory_space=pltpu.VMEM), pl.BlockSpec(memory_space=pl.ANY),
                  pl.BlockSpec(memory_space=pl.ANY)],
        out_specs=pl.BlockSpec(memory_space=pl.ANY),
        scratch_shapes=scratch,
        compiler_params=pltpu.CompilerParams(
            collective_id=0, has_side_effects=True, vmem_limit_bytes=56 * 1024 * 1024),
        name="sinkhorn",
    )(embeddings, centroids, plan_grad)


def fast_shards(embeddings, centroids, plan_grad):
    n = lax.axis_size("prog")
    rows, depth = embeddings.shape
    scale = 1.0 / (0.25 * depth**0.5)
    ratio = rows * n / centroids.shape[0]
    adjoint_b = adjoint_of(n, scale, ratio, embeddings, centroids, plan_grad)
    part = scale * lax.dot_general(
        adjoint_b, embeddings, (((0,), (0,)), ((), ())), preferred_element_type=jnp.float32)
    centroid_grad = lax.psum_scatter(
        part, "prog", scatter_dimension=0, tiled=True).astype(jnp.bfloat16)
    embed_grad = (scale * jnp.dot(
        adjoint_b, centroids, preferred_element_type=jnp.float32)).astype(jnp.bfloat16)
    return (embed_grad, centroid_grad)


def solution(mesh):
    fast = mesh.shape["clus"] == 1 and ITERS == 4
    placed = (P("prog", "clus"), P("clus", None), P("prog", "clus"))
    return jax.shard_map(
        fast_shards if fast else general_shards,
        mesh=mesh,
        in_specs=placed,
        out_specs=(P("prog", "clus"), P(("clus", "prog"), None)),
        check_vma=False,
    )
```

```python
import functools

import jax
import jax.numpy as jnp
from jax import lax
from jax.experimental import pallas as pl
from jax.experimental.pallas import tpu as pltpu
from jax.sharding import PartitionSpec as P

ITERS = 4


def merged(part, axis, combine):
    gathered = jax.tree.map(lambda a: lax.all_gather(a, axis), part)

    def take(source):
        return jax.tree.map(lambda a: lax.dynamic_index_in_dim(a, source, 0, False), gathered)

    return lax.fori_loop(
        1, lax.axis_size(axis), lambda source, state: combine(state, take(source)), take(0)
    )


def lse_combine(first, second):
    top = jnp.maximum(first[0], second[0])
    total = first[1] * jnp.exp(first[0] - top) + second[1] * jnp.exp(second[0] - top)
    return (top, total)


def row_lse(values):
    local_top = jnp.max(values, axis=1)
    local_total = jnp.sum(jnp.exp(values - local_top[:, None]), axis=1)
    top, total = merged((local_top, local_total), "clus", lse_combine)
    return top + jnp.log(total)


def col_lse(values):
    local_top = jnp.max(values, axis=0)
    local_total = jnp.sum(jnp.exp(values - local_top[None, :]), axis=0)
    top, total = merged((local_top, local_total), "prog", lse_combine)
    return top + jnp.log(total)


def general_shards(embeddings, centroids, plan_grad):
    scale = 1.0 / (0.25 * jnp.sqrt(jnp.float32(embeddings.shape[1] * lax.axis_size("clus"))))
    whole_rows = lax.all_gather(embeddings, "clus", axis=1, tiled=True)
    logits = scale * lax.dot_general(
        whole_rows, centroids, (((1,), (1,)), ((), ())), preferred_element_type=jnp.float32
    )
    total_rows = embeddings.shape[0] * lax.axis_size("prog")
    log_b = jnp.log(jnp.float32(total_rows) / jnp.float32(centroids.shape[0] * lax.axis_size("clus")))
    col_pot = jnp.zeros((centroids.shape[0],), jnp.float32)
    row_list = []
    col_list = []
    for step in range(ITERS):
        row_pot = -row_lse(logits + col_pot[None, :])
        col_pot = log_b - col_lse(logits + row_pot[:, None])
        row_list.append(row_pot)
        col_list.append(col_pot)
    plan = jnp.exp(logits + row_list[-1][:, None] + col_list[-1][None, :])
    pbar = plan_grad.astype(jnp.float32) * plan
    adjoint = pbar
    col_adj = lax.psum(jnp.sum(pbar, axis=0), "prog")
    direct = jnp.sum(pbar, axis=1)
    for step in range(ITERS - 1, -1, -1):
        weights_a = jnp.exp(logits + row_list[step][:, None] + col_list[step][None, :] - log_b)
        term_a = weights_a * col_adj[None, :]
        adjoint = adjoint - term_a
        row_adj = lax.psum(direct - jnp.sum(term_a, axis=1), "clus")
        direct = jnp.zeros_like(direct)
        if step > 0:
            prev_col = col_list[step - 1]
        else:
            prev_col = jnp.zeros_like(col_pot)
        term_b = jnp.exp(logits + prev_col[None, :] + row_list[step][:, None]) * row_adj[:, None]
        adjoint = adjoint - term_b
        if step > 0:
            col_adj = -lax.psum(jnp.sum(term_b, axis=0), "prog")
    adjoint_b = adjoint.astype(jnp.bfloat16)
    partial_rows = scale * jnp.dot(adjoint_b, centroids, preferred_element_type=jnp.float32)
    embed_grad = lax.psum_scatter(partial_rows, "clus", scatter_dimension=1, tiled=True).astype(
        jnp.bfloat16
    )
    centroid_grad = lax.psum_scatter(
        scale
        * lax.dot_general(
            adjoint_b, whole_rows, (((0,), (0,)), ((), ())), preferred_element_type=jnp.float32
        ),
        "prog",
        scatter_dimension=0,
        tiled=True,
    ).astype(jnp.bfloat16)
    return (embed_grad, centroid_grad)


LANES = 128
MESH_AXIS = "prog"


def sinkhorn_kernel(
    n, scale, ratio, emb, cent, grad, out,
    E, G, tiles, A, X, R, U, sub, cols, RW, RH, LH,
    send1, got1, reply1, back1, send2, got2, reply2, back2,
    tile_sem, grad_sem, out_sem, ss1, rs1, ss2, rs2,
):
    rows, C = E.shape
    W = C // n
    K = C // LANES
    me = lax.axis_index(MESH_AXIS)
    f32 = jnp.float32

    def other(k):
        return lax.rem(me + k, n)

    barrier = pltpu.get_barrier_semaphore()

    @pl.loop(1, n)
    def _(k):
        pl.semaphore_signal(barrier, inc=1, device_id={MESH_AXIS: other(k)},
                            device_id_type=pl.DeviceIdType.MESH)

    grad_copy = pltpu.make_async_copy(grad, G, grad_sem)
    width = tiles.shape[1]
    count = C // width

    def fetch(j):
        return pltpu.make_async_copy(
            cent.at[pl.ds(j * width, width), :], tiles.at[j % 2], tile_sem.at[j % 2])

    fetch(0).start()
    for j in range(count):
        if j + 1 < count:
            fetch(j + 1).start()
        if j == 0:
            grad_copy.start()
        fetch(j).wait()

        half = rows // 4

        @pl.loop(0, 4)
        def _(q, j=j):
            r0 = pl.multiple_of(q * half, half)
            E[pl.ds(r0, half), j * width:(j + 1) * width] = scale * lax.dot_general(
                emb[pl.ds(r0, half), :], tiles[j % 2], (((1,), (1,)), ((), ())),
                preferred_element_type=f32)

    pl.semaphore_wait(barrier, n - 1)

    BR = 64
    BC = 16
    CH = 8

    def rows_loop(body):
        @pl.loop(0, rows // BR)
        def _(i):
            body(pl.ds(pl.multiple_of(i * BR, BR), BR))

    def lane(k):
        return slice(k * LANES, (k + 1) * LANES)

    def cols_loop(body, init, outs, combine):
        for c in range(K // CH):
            def step(i, accs, c=c):
                r = pl.ds(pl.multiple_of(i * BC, BC), BC)
                new = []
                for q in range(CH):
                    terms = body(r, c * CH + q)
                    new.append(tuple(combine(a, t) for a, t in zip(accs[q], terms)))
                return tuple(new)

            start = tuple(
                tuple(jnp.full((BC, LANES), init, f32) for _ in outs) for _ in range(CH))
            accs = lax.fori_loop(0, rows // BC, step, start, unroll=2)
            for q in range(CH):
                for o, a in zip(outs, accs[q]):
                    if combine is jnp.maximum:
                        red = jnp.max(a, axis=0, keepdims=True)
                    else:
                        red = jnp.sum(a, axis=0, keepdims=True)
                    o[:, lane(c * CH + q)] = red

    def total(part):
        return jnp.broadcast_to(jnp.sum(part, axis=1, keepdims=True), part.shape)

    def row_pass(y):
        def body(r):
            acc = E[r, lane(0)] * y[:, lane(0)]
            for k in range(1, K):
                acc = acc + E[r, lane(k)] * y[:, lane(k)]
            R[r, :] = acc
        rows_loop(body)

    def exchange(vectors, combine, results, send, got, reply, back):
        for k in range(n):
            for q, v in enumerate(vectors):
                send[k, :, q * W:(q + 1) * W] = v[:, k * W:(k + 1) * W]

        def first(k):
            t = other(k)
            return pltpu.make_async_remote_copy(
                src_ref=send.at[t], dst_ref=got.at[me], send_sem=ss1.at[t],
                recv_sem=rs1.at[me], device_id={MESH_AXIS: t},
                device_id_type=pl.DeviceIdType.MESH)

        def first_in(k):
            t = other(k)
            return pltpu.make_async_remote_copy(
                src_ref=send.at[t], dst_ref=got.at[t], send_sem=ss1.at[t],
                recv_sem=rs1.at[t], device_id={MESH_AXIS: t},
                device_id_type=pl.DeviceIdType.MESH)

        def second(k):
            t = other(k)
            return pltpu.make_async_remote_copy(
                src_ref=reply, dst_ref=back.at[me], send_sem=ss2.at[t],
                recv_sem=rs2.at[me], device_id={MESH_AXIS: t},
                device_id_type=pl.DeviceIdType.MESH)

        def second_in(k):
            t = other(k)
            return pltpu.make_async_remote_copy(
                src_ref=reply, dst_ref=back.at[t], send_sem=ss2.at[t],
                recv_sem=rs2.at[t], device_id={MESH_AXIS: t},
                device_id_type=pl.DeviceIdType.MESH)

        @pl.loop(1, n)
        def _(k):
            first(k).start()

        got[me] = send[me]

        @pl.loop(1, n)
        def _(k):
            first_in(k).wait_recv()

        arrived = got[...]
        answers = combine([arrived[:, :, q * W:(q + 1) * W] for q in range(len(vectors))])
        for q, a in enumerate(answers):
            reply[:, q * W:(q + 1) * W] = a

        @pl.loop(1, n)
        def _(k):
            second(k).start()

        back[me] = reply[...]

        @pl.loop(1, n)
        def _(k):
            first(k).wait_send()
            second_in(k).wait_recv()

        for k in range(n):
            for q, v in enumerate(results):
                v[:, k * W:(k + 1) * W] = back[k, :, q * W:(q + 1) * W]

        @pl.loop(1, n)
        def _(k):
            second(k).wait_send()

    M, F = cols.at[pl.ds(0, 1)], cols.at[pl.ds(1, 1)]
    B = {t: cols.at[pl.ds(t, 1)] for t in (2, 3, 4)}
    DV = cols.at[pl.ds(5, 1)]
    Y, Y2, S, S2, EM = (cols.at[pl.ds(q, 1)] for q in (8, 9, 10, 11, 12))

    def top_body(r):
        acc = E[r, lane(0)]
        for k in range(1, K):
            acc = jnp.maximum(acc, E[r, lane(k)])
        R[r, :] = jnp.broadcast_to(jnp.max(acc, axis=1, keepdims=True), acc.shape)

    rows_loop(top_body)

    def exp_body(r):
        top = R[r, :]
        acc = jnp.exp(E[r, lane(0)] - top)
        for k in range(1, K):
            acc = acc + jnp.exp(E[r, lane(k)] - top)
        U[r, :] = -(top + jnp.log(total(acc)))

    rows_loop(exp_body)
    cols_loop(lambda r, k: [E[r, lane(k)] + U[r, :]], -jnp.inf, [M], jnp.maximum)

    def shift(r, k):
        e = jnp.exp(E[r, lane(k)] + U[r, :] - M[:, lane(k)])
        E[r, lane(k)] = e
        return [e]

    add = lambda a, b: a + b
    cols_loop(shift, 0.0, [S], add)

    def lse(parts):
        m, s = parts
        top = jnp.max(m, axis=0)
        whole = jnp.sum(s * jnp.exp(m - top[None]), axis=0)
        v = jnp.log(f32(ratio)) - (top + jnp.log(whole))
        return [v, v]

    exchange([M, S], lse, [Y], send2, got2, reply2, back2)
    F[...] = jnp.exp(M[...] + Y[...])
    EM[...] = jnp.exp(M[...])

    def plain(parts):
        return [jnp.sum(p, axis=0) for p in parts]

    def fb(t):
        if t == 0:
            return EM[...]
        return F[...] if t == 1 else F[...] * B[t][...]

    A[0] = jnp.ones((rows, LANES), f32)
    for t in (2, 3, 4):
        Y[...] = fb(t - 1)
        row_pass(Y)
        A[t - 1] = 1.0 / total(R[...])
        if t < 4:
            cols_loop(lambda r, k, t=t: [E[r, lane(k)] * A[t - 1, r, :]], 0.0, [S], add)
            S[...] = S[...] * F[...]
            exchange([S], plain, [Y], send1, got1, reply1, back1)
            B[t][...] = ratio / Y[...]
        else:
            grad_copy.wait()

            def both(r, k):
                w = E[r, lane(k)] * A[3, r, :]
                return [w, w * G[r, lane(k)].astype(f32)]

            cols_loop(both, 0.0, [S, S2], add)
            S[...] = S[...] * F[...]
            S2[...] = S2[...] * F[...]
            exchange([S, S2], plain, [Y, Y2], send2, got2, reply2, back2)
            B[t][...] = ratio / Y[...]
            DV[...] = B[t][...] * Y2[...]

    for t in (4, 3, 2, 1):
        Y[...] = fb(t) * DV[...] * (1.0 / ratio)
        RW[t - 1:t, :] = Y[...]
        RW[3 + t:4 + t, :] = fb(t - 1)
        if t == 4:
            Y2[...] = fb(4)

            def grad_body(r):
                acc = jnp.zeros((BR, LANES), f32)
                for k in range(K):
                    acc = acc + E[r, lane(k)] * (
                        G[r, lane(k)].astype(f32) * Y2[:, lane(k)] - Y[:, lane(k)])
                R[r, :] = acc

            rows_loop(grad_body)
            X[t - 1] = A[t - 1] * A[t - 1] * total(R[...])
        else:
            row_pass(Y)
            X[t - 1] = -(A[t - 1] * A[t - 1]) * total(R[...])
        if t > 1:
            cols_loop(lambda r, k, t=t: [E[r, lane(k)] * X[t - 1, r, :]], 0.0, [S], add)
            S[...] = S[...] * F[...]
            exchange([S], plain, [Y], send1, got1, reply1, back1)
            if t == 2:
                DV[...] = -Y[...]
            else:
                DV[...] = -Y[...] * B[t - 1][...]

    high = RW[...].astype(jnp.bfloat16).astype(f32)
    low = RW[...] - high
    RH[...] = jnp.concatenate(
        [high, low, high, jnp.zeros_like(high)], axis=0).astype(jnp.bfloat16)
    spot = lax.broadcasted_iota(jnp.int32, (BR, LANES), 1)

    def left(r):
        acc = jnp.zeros((BR, LANES), f32)
        for q in range(8):
            v = A[q, r, :] if q < 4 else X[q - 4, r, :]
            hi = v.astype(jnp.bfloat16).astype(f32)
            acc = jnp.where((spot == q) | (spot == q + 8), hi, acc)
            acc = jnp.where(spot == q + 16, v - hi, acc)
        LH[r, :] = acc.astype(jnp.bfloat16)

    rows_loop(left)
    Y2[...] = fb(4)

    def finish(r):
        lhs = LH[r, :][:, 0:32]
        a4 = A[3, r, :]
        for k in range(0, K, 2):
            wide = slice(k * LANES, (k + 2) * LANES)
            coef = jnp.dot(lhs, RH[:, wide], preferred_element_type=f32)
            a = jnp.concatenate([a4, a4], axis=1)
            val = E[r, wide] * (G[r, wide].astype(f32) * a * Y2[:, wide] - coef)
            G[r, wide] = val.astype(jnp.bfloat16)

    rows_loop(finish)
    done = pltpu.make_async_copy(G, out, out_sem)
    done.start()
    done.wait()


def adjoint_of(n, scale, ratio, embeddings, centroids, plan_grad):
    rows, depth = embeddings.shape
    C = centroids.shape[0]
    W = C // n
    f32 = jnp.float32
    width = 512
    vm = pltpu.VMEM
    scratch = [
        vm((rows, C), f32), vm((rows, C), jnp.bfloat16), vm((2, width, depth), jnp.bfloat16),
        vm((4, rows, LANES), f32), vm((4, rows, LANES), f32), vm((rows, LANES), f32),
        vm((rows, LANES), f32), vm((8, LANES), f32), vm((16, C), f32),
        vm((8, C), f32), vm((32, C), jnp.bfloat16), vm((rows, LANES), jnp.bfloat16),
        vm((n, 1, W), f32), vm((n, 1, W), f32), vm((1, W), f32), vm((n, 1, W), f32),
        vm((n, 1, 2 * W), f32), vm((n, 1, 2 * W), f32), vm((1, 2 * W), f32),
        vm((n, 1, 2 * W), f32),
        pltpu.SemaphoreType.DMA((2,)), pltpu.SemaphoreType.DMA, pltpu.SemaphoreType.DMA,
        pltpu.SemaphoreType.DMA((n,)), pltpu.SemaphoreType.DMA((n,)),
        pltpu.SemaphoreType.DMA((n,)), pltpu.SemaphoreType.DMA((n,)),
    ]
    return pl.pallas_call(
        functools.partial(sinkhorn_kernel, n, scale, ratio),
        out_shape=jax.ShapeDtypeStruct((rows, C), jnp.bfloat16),
        in_specs=[pl.BlockSpec(memory_space=pltpu.VMEM), pl.BlockSpec(memory_space=pl.ANY),
                  pl.BlockSpec(memory_space=pl.ANY)],
        out_specs=pl.BlockSpec(memory_space=pl.ANY),
        scratch_shapes=scratch,
        compiler_params=pltpu.CompilerParams(
            collective_id=0, has_side_effects=True, vmem_limit_bytes=56 * 1024 * 1024),
        name="sinkhorn",
    )(embeddings, centroids, plan_grad)


SUBS = 8


def grads_kernel(
    n, scale, adj_in, emb, cent, eg_out, cg_out,
    adj, ebuf, embt, cbuf, obuf, own, send, got0, got1, got2, got3, got4,
    adj_sem, emb_sem, cent_sem, out_sem, ss, rs,
):
    gots = (got0, got1, got2, got3, got4)
    f32, b16 = jnp.float32, jnp.bfloat16
    rows, C = adj.shape
    depth = emb.shape[1]
    sub = depth // SUBS
    me = lax.axis_index(MESH_AXIS)
    core = lax.rem(me, 2)
    mine_q = me // 2
    nb = len(gots) - 1
    orders = {0: (0, 1, 2, 3), 1: (1, 0, 2, 3), 2: (2, 3, 0, 1)}
    kinds = (0, 1, 2, 0, 1, 0, 1, 2)

    def bit(v, b):
        return lax.rem(v // (1 << b), 2)

    def partner(b):
        return me + (1 << b) * (1 - 2 * bit(me, b))

    barrier = pltpu.get_barrier_semaphore()
    for b in range(nb + 1):
        pl.semaphore_signal(barrier, inc=1, device_id={MESH_AXIS: partner(b)},
                            device_id_type=pl.DeviceIdType.MESH)

    adj_copy = pltpu.make_async_copy(adj_in, adj, adj_sem)
    adj_copy.start()

    def emb_copy(c):
        return pltpu.make_async_copy(
            emb.at[:, pl.ds(c * 2 * sub, 2 * sub)], ebuf.at[c % 2], emb_sem.at[c % 2])

    def cent_copy(c):
        return pltpu.make_async_copy(
            cent.at[:, pl.ds(c * sub, sub)], cbuf.at[c % 2], cent_sem.at[c % 2])

    def out_copy(c):
        return pltpu.make_async_copy(
            obuf.at[c % 2], eg_out.at[:, pl.ds(c * sub, sub)], out_sem.at[c % 2])

    heads = n // 2

    def span(l):
        if l == 0:
            return (0, heads)
        size = heads >> l
        return (heads - 2 * size, size)

    def transfer(s, l):
        at, size = span(l)
        b = 0 if l == 0 else orders[kinds[s]][l - 1] + 1
        return pltpu.make_async_remote_copy(
            src_ref=send.at[s, pl.ds(at, size)], dst_ref=gots[l].at[s],
            send_sem=ss.at[s, l], recv_sem=rs.at[s, l],
            device_id={MESH_AXIS: partner(b)}, device_id_type=pl.DeviceIdType.MESH)

    def level(s, l):
        order = orders[kinds[s]]
        transfer(s, l - 1).wait_recv()
        if l == 1:
            transfer(s, 0).wait_send()
        fixed = 0
        for b in order[:l - 1]:
            fixed = fixed + (1 << b) * bit(mine_q, b)
        free = order[l:]
        here = order[l - 1]
        mine_bit = bit(mine_q, here)
        at, size = span(l)
        got = gots[l - 1]

        @pl.loop(0, size)
        def _(i):
            base = fixed
            for j, b in enumerate(free):
                base = base + (1 << b) * bit(i, j)
            away = base + (1 << here) * (1 - mine_bit)
            keep = base + (1 << here) * mine_bit
            if l == 1:
                away_at, keep_at = away, keep
            else:
                away_at = 2 * i + 1 - mine_bit
                keep_at = 2 * i + mine_bit
            send[s, at + i] = (own[s, away] + got[s, away_at].astype(f32)).astype(b16)
            own[s, keep] = own[s, keep] + got[s, keep_at].astype(f32)

        transfer(s, l).start()

    def last(s):
        transfer(s, nb).wait_recv()
        whole = own[s, mine_q] + gots[nb][s, 0].astype(f32)
        cg_out[:, s * sub:(s + 1) * sub] = (scale * whole.T).astype(b16)

    group = 4 * LANES

    def partial(c):
        emb_copy(c).wait()
        embt[...] = ebuf[c % 2].T
        if c + 2 < SUBS // 2:
            emb_copy(c + 2).start()

        @pl.loop(0, C // group)
        def _(g):
            res = jnp.dot(embt[...], adj[:, pl.ds(pl.multiple_of(g * group, group), group)],
                          preferred_element_type=f32)
            for qq in range(2):
                r0 = res[:, 2 * qq * LANES:(2 * qq + 1) * LANES]
                r1 = res[:, (2 * qq + 1) * LANES:(2 * qq + 2) * LANES]
                kept = jnp.where(core == 0, r0, r1)
                away = jnp.where(core == 0, r1, r0).astype(b16)
                for h in range(2):
                    own[2 * c + h, 2 * g + qq] = kept[h * sub:(h + 1) * sub]
                    send[2 * c + h, 2 * g + qq] = away[h * sub:(h + 1) * sub]

        if c == 0:
            pl.semaphore_wait(barrier, nb + 1)
        transfer(2 * c, 0).start()
        transfer(2 * c + 1, 0).start()

    block = rows // 2

    def embed(c):
        cent_copy(c).wait()
        if c >= 2:
            out_copy(c - 2).wait()

        @pl.loop(0, rows // block)
        def _(q):
            r = pl.ds(pl.multiple_of(q * block, block), block)
            obuf[c % 2, r, :] = (scale * jnp.dot(
                adj[r, :], cbuf[c % 2], preferred_element_type=f32)).astype(b16)

        out_copy(c).start()
        if c + 2 < SUBS:
            cent_copy(c + 2).start()

    emb_copy(0).start()
    emb_copy(1).start()
    cent_copy(0).start()
    cent_copy(1).start()
    adj_copy.wait()
    partial(0)
    partial(1)
    level(0, 1)
    level(1, 1)
    partial(2)
    level(2, 1)
    level(3, 1)
    partial(3)
    level(4, 1)
    level(5, 1)
    embed(0)
    level(6, 1)
    level(7, 1)
    level(0, 2)
    level(1, 2)
    embed(1)
    level(2, 2)
    embed(2)
    level(3, 2)
    level(4, 2)
    embed(3)
    level(0, 3)
    level(1, 3)
    embed(4)
    level(2, 3)
    level(7, 2)
    embed(5)
    level(5, 2)
    level(6, 2)
    embed(6)
    level(3, 3)
    level(4, 3)
    level(0, 4)
    level(1, 4)
    embed(7)
    for s, l in ((2, 4), (7, 3), (5, 3), (6, 3), (3, 4), (4, 4), (7, 4), (5, 4), (6, 4)):
        level(s, l)
    for s in (0, 1, 2, 3, 4, 7, 5, 6):
        last(s)
    for s in range(SUBS):
        for l in range(1, nb + 1):
            transfer(s, l).wait_send()
    out_copy(SUBS - 2).wait()
    out_copy(SUBS - 1).wait()


def grads_of(n, scale, adjoint_b, embeddings, centroids):
    rows, C = adjoint_b.shape
    depth = embeddings.shape[1]
    sub = depth // SUBS
    heads = n // 2
    b16, f32 = jnp.bfloat16, jnp.float32
    vm = pltpu.VMEM
    dma = pltpu.SemaphoreType.DMA
    levels = n.bit_length() - 1
    scratch = [
        vm((rows, C), b16), vm((2, rows, 2 * sub), b16), vm((2 * sub, rows), b16),
        vm((2, C, sub), b16), vm((2, rows, sub), b16),
        vm((SUBS, heads, sub, LANES), f32), vm((SUBS, heads, sub, LANES), b16),
    ]
    scratch += [vm((SUBS, heads >> l, sub, LANES), b16) for l in range(levels)]
    scratch += [dma, dma((2,)), dma((2,)), dma((2,)), dma((SUBS, levels)), dma((SUBS, levels))]
    return pl.pallas_call(
        functools.partial(grads_kernel, n, scale),
        out_shape=(jax.ShapeDtypeStruct((rows, depth), b16),
                   jax.ShapeDtypeStruct((C // n, depth), b16)),
        in_specs=[pl.BlockSpec(memory_space=pl.ANY)] * 3,
        out_specs=(pl.BlockSpec(memory_space=pl.ANY), pl.BlockSpec(memory_space=pltpu.VMEM)),
        scratch_shapes=scratch,
        compiler_params=pltpu.CompilerParams(
            collective_id=1, has_side_effects=True, vmem_limit_bytes=62 * 1024 * 1024),
        name="grads",
    )(adjoint_b, embeddings, centroids)


def fast_shards(embeddings, centroids, plan_grad):
    n = lax.axis_size("prog")
    rows, depth = embeddings.shape
    scale = 1.0 / (0.25 * depth**0.5)
    ratio = rows * n / centroids.shape[0]
    adjoint_b = adjoint_of(n, scale, ratio, embeddings, centroids, plan_grad)
    return grads_of(n, scale, adjoint_b, embeddings, centroids)


def solution(mesh):
    fast = mesh.shape["clus"] == 1 and mesh.shape["prog"] == 32
    placed = (P("prog", "clus"), P("clus", None), P("prog", "clus"))
    return jax.shard_map(
        fast_shards if fast else general_shards,
        mesh=mesh,
        in_specs=placed,
        out_specs=(P("prog", "clus"), P(("clus", "prog"), None)),
        check_vma=False,
    )
```
